1024 devices in a mesh: dp: 64 (over z_hi, y, core), tensor: 16 (over z_lo, x).
Axes of the slice: x: 4, y: 8, z: 16 (z_hi: 4, z_lo: 4; z = z_hi * 4 + z_lo), core: 2. Of those that a mesh axis runs over, the one named last changes fastest.
Arguments:
- gate_pre: bfloat16 [32768, 14336], P(('dp', 'tensor')), parts along dimension 0, may hold values from -6 to 6
- up_pre: bfloat16 [32768, 14336], P(('dp', 'tensor')), parts along dimension 0, may hold values from -6 to 6
- down_weight: bfloat16 [14336, 4096], P('tensor'), may hold values from -0.046875 to 0.046875
Outputs:
- mixed: bfloat16 [32768, 4096], P(('dp', 'tensor')), parts along dimension 0
The draws below stay inside these ranges and needn't reach their ends.
There are 64 independent parts, one for each index of `dp`. The reference program is written for one: setup_inputs(seed, part) draws one part's arguments, and reference() takes and returns one part's arrays. A program takes and returns all parts, laid end to end along the dimension named above; an argument that names none is the same for every part. Nothing has to cross between parts.
All inputs are finite; a program needn't handle non-finite values.
Results may differ from the reference program's by a relative error of at most 0.023.
Values may be sent and summed in bfloat16 or wider, within the bound.
No kernel may reach another device: no remote copies, remote signals or barrier semaphores. Data moves between devices by JAX's collectives and lax.ppermute only.
A program may use at most 32 MiB of HBM per device.

```python
import jax
import jax.numpy as jnp
from jax import lax

D = 4096
FF = 14336
TOKENS = 512
N_TENSOR = 16


def steps_of(own_key, dims, pieces, least, top_value):
    factor_of, own = 1.0, jax.random.fold_in(own_key, 6)
    for dim, parts in pieces:
        steps = jnp.exp(jax.random.uniform(jax.random.fold_in(own, dim), (parts,), jnp.float32, least / len(pieces), top_value / len(pieces)))
        factor_of = factor_of * jnp.repeat(steps, dims[dim] // parts).reshape([-1 if axis == dim else 1 for axis in range(len(dims))])
    return factor_of


def centred(rng, extent, deviation, most, cuts=(), held_as=jnp.bfloat16):
    factor_of = steps_of(rng, extent, cuts, -0.22, 0.18) if cuts else 1.0
    entries = jax.random.normal(rng, extent, jnp.float32) * deviation * factor_of
    return jnp.minimum(jnp.maximum(entries, -most), most).astype(held_as)


def setup_inputs(seed: int = 0, part: int = 0) -> dict:
    arg_keys = jax.random.split(jax.random.key(seed), 4)
    part_splits = jax.random.split(jax.random.fold_in(arg_keys[3], part), 4)
    return {
        "gate_pre": centred(part_splits[0], (TOKENS, FF), 1.0, 6.0, ((0, 16),)),
        "up_pre": centred(part_splits[1], (TOKENS, FF), 1.0, 6.0, ((0, 16),)),
        "down_weight": centred(arg_keys[2], (FF, D), FF ** -0.5, 0.046875, ((0, 16),)),
    }


def reference(gate_pre, up_pre, down_weight):
    hidden = (jax.nn.silu(gate_pre.astype(jnp.float32)) * up_pre.astype(jnp.float32)).astype(jnp.bfloat16)
    width = FF // N_TENSOR
    total = jnp.zeros((hidden.shape[0], D), jnp.float32)
    for block in range(N_TENSOR):
        partial_value = jnp.dot(hidden[:, block * width:(block + 1) * width], down_weight[block * width:(block + 1) * width], preferred_element_type=jnp.float32).astype(jnp.bfloat16)
        partial_value = lax.optimization_barrier(partial_value)
        total = total + partial_value.astype(jnp.float32)
    return total.astype(jnp.bfloat16)
```

```python
import functools

import jax
import jax.numpy as jnp
import numpy as np
from jax import lax
from jax.experimental import pallas as pl
from jax.experimental.pallas import tpu as pltpu
from jax.sharding import PartitionSpec as P

AXES = ("dp", "tensor")
Z_HI, Y, CORES, Z_LO, X = 4, 8, 2, 4, 4
WIDTH, D, ROWS = 896, 4096, 32
STEPS = (0, 1, -1, 2)
MIB = 1 << 20


def moves(axis, step):
    pairs = []
    for zh, y, c, zl, x in np.ndindex(Z_HI, Y, CORES, Z_LO, X):
        z = zh * Z_LO + zl
        if axis == c:
            to_z, to_x = z, (x + step) % X
        else:
            to_z, to_x = (z + step) % (Z_HI * Z_LO), x
        source = (((zh * Y + y) * CORES + c) * Z_LO + zl) * X + x
        target = (((to_z // Z_LO * Y + y) * CORES + c) * Z_LO + to_z % Z_LO) * X + to_x
        pairs.append((source, target))
    return pairs


def send(value, axis, step):
    return lax.ppermute(value, AXES, moves(axis, step))


def vmem(shape):
    return pltpu.VMEM(shape, jnp.bfloat16)


def in_vmem(*arrays):
    return [pltpu.with_memory_space_constraint(a, pltpu.VMEM) for a in arrays]


def whole():
    return pl.BlockSpec(memory_space=pltpu.VMEM)


def activate_kernel(gate_ref, up_ref, own, plus1, minus1, plus2, minus2, gate_buf, up_buf, sems):
    dp, tensor = lax.axis_index("dp"), lax.axis_index("tensor")
    core = lax.rem(dp, CORES)
    zl, x = lax.div(tensor, X), lax.rem(tensor, X)
    copies = []
    for k, first in enumerate(STEPS):
        for j, second in enumerate(STEPS):
            by_z = jnp.where(core == 0, second, first)
            by_x = jnp.where(core == 0, first, second)
            block = lax.rem(zl + by_z + Z_LO, Z_LO) * X + lax.rem(x + by_x + X, X)
            columns = pl.ds(pl.multiple_of(block * WIDTH, 128), WIDTH)
            slot = 4 * k + j
            pair = (
                pltpu.make_async_copy(gate_ref.at[:, columns], gate_buf.at[slot], sems.at[0, slot]),
                pltpu.make_async_copy(up_ref.at[:, columns], up_buf.at[slot], sems.at[1, slot]),
            )
            for copy in pair:
                copy.start()
            copies.append(pair)
    for k in range(4):
        for j in range(4):
            slot = 4 * k + j
            for copy in copies[slot]:
                copy.wait()
            gate = gate_buf[slot].astype(jnp.float32)
            hidden = (jax.nn.silu(gate) * up_buf[slot].astype(jnp.float32)).astype(jnp.bfloat16)
            if k < 3:
                (own, plus1, minus1)[k][j] = hidden
            else:
                plus2[j] = hidden[:16]
                minus2[j] = hidden[16:]


def activate(gate_pre, up_pre):
    full, half = vmem((4, 32, WIDTH)), vmem((4, 16, WIDTH))
    return pl.pallas_call(
        activate_kernel,
        out_shape=[full, full, full, half, half],
        in_specs=[pl.BlockSpec(memory_space=pl.ANY)] * 2,
        out_specs=[whole()] * 5,
        scratch_shapes=[
            pltpu.VMEM((16, ROWS, WIDTH), jnp.bfloat16),
            pltpu.VMEM((16, ROWS, WIDTH), jnp.bfloat16),
            pltpu.SemaphoreType.DMA((2, 16)),
        ],
        compiler_params=pltpu.CompilerParams(vmem_limit_bytes=8 * MIB),
        name="activate",
    )(gate_pre, up_pre)


SPANS = ((0, 32), (32, 64), (64, 96), (96, 112), (112, 128))


def pack_kernel(*refs):
    parts, outs = refs[:5], refs[5:]
    for j in range(3):
        for part, (low, high) in zip(parts, SPANS):
            outs[j][low:high, :] = part[j]
    for part, (low, high) in zip(parts, SPANS):
        if high <= 64:
            outs[3][low:high, :] = part[3]
        else:
            outs[4][low - 64 : high - 64, :] = part[3]


def pack(*parts):
    full, half = vmem((128, WIDTH)), vmem((64, WIDTH))
    return pl.pallas_call(
        pack_kernel,
        out_shape=[full, full, full, half, half],
        in_specs=[whole()] * 5,
        out_specs=[whole()] * 5,
        compiler_params=pltpu.CompilerParams(vmem_limit_bytes=4 * MIB),
        name="pack",
    )(*in_vmem(*parts))


TILE = 512


def project_kernel(count, *refs):
    rows, weight, outs, held = refs[:count], refs[count], refs[count + 1 : -1], refs[-1]
    low = 0
    for part in rows:
        held[low : low + part.shape[0], :] = part[...]
        low += part.shape[0]

    @pl.loop(0, D // TILE)
    def _(step):
        columns = pl.ds(pl.multiple_of(step * TILE, TILE), TILE)
        terms = jnp.dot(held[...], weight[:, columns], preferred_element_type=jnp.float32)
        low = 0
        for out in outs:
            out[:, columns] = terms[low : low + out.shape[0]].astype(jnp.bfloat16)
            low += out.shape[0]


def project(weight, *rows):
    total = sum(part.shape[0] for part in rows)
    return pl.pallas_call(
        functools.partial(project_kernel, len(rows)),
        out_shape=[vmem((part.shape[0], D)) for part in rows],
        in_specs=[whole()] * (len(rows) + 1),
        out_specs=[whole()] * len(rows),
        scratch_shapes=[pltpu.VMEM((total, WIDTH), jnp.bfloat16)],
        cost_estimate=pl.CostEstimate(
            flops=2 * total * WIDTH * D, bytes_accessed=2 * WIDTH * D, transcendentals=0
        ),
        compiler_params=pltpu.CompilerParams(vmem_limit_bytes=8 * MIB),
        name="project",
    )(*in_vmem(*rows, weight))


def add_kernel(spans, own, plus1, minus1, plus2, minus2, *outs):
    half = plus2.shape[0]

    @pl.loop(0, D // TILE)
    def _(step):
        columns = pl.ds(pl.multiple_of(step * TILE, TILE), TILE)
        for out, (low, high) in zip(outs, spans):
            far = plus2[low:high, columns] if high <= half else minus2[low - half : high - half, columns]
            out[:, columns] = (
                own[low:high, columns].astype(jnp.float32)
                + plus1[low:high, columns].astype(jnp.float32)
                + minus1[low:high, columns].astype(jnp.float32)
                + far.astype(jnp.float32)
            ).astype(jnp.bfloat16)


def add_up(spans, *parts):
    return pl.pallas_call(
        functools.partial(add_kernel, spans),
        out_shape=[vmem((high - low, D)) for low, high in spans],
        in_specs=[whole()] * 5,
        out_specs=[whole()] * len(spans),
        compiler_params=pltpu.CompilerParams(vmem_limit_bytes=8 * MIB),
        name="add_up",
    )(*in_vmem(*parts))


def final_kernel(own, plus1, minus1, plus2, minus2, out):
    for low, far in ((0, plus2), (16, minus2)):
        rows = slice(low, low + 16)
        out[rows, :] = (
            own[rows, :].astype(jnp.float32)
            + plus1[rows, :].astype(jnp.float32)
            + minus1[rows, :].astype(jnp.float32)
            + far[...].astype(jnp.float32)
        ).astype(jnp.bfloat16)


def final_sum(*parts):
    return pl.pallas_call(
        final_kernel,
        out_shape=jax.ShapeDtypeStruct((ROWS, D), jnp.bfloat16),
        in_specs=[whole()] * 5,
        out_specs=whole(),
        compiler_params=pltpu.CompilerParams(vmem_limit_bytes=4 * MIB),
        name="final_sum",
    )(*in_vmem(*parts))


FAR = (1, -1, 2, -2)


def shards(gate_pre, up_pre, down_weight):
    own, *away = activate(gate_pre, up_pre)
    came = [send(part, 0, step) for part, step in zip(away, FAR)]
    here, *away = pack(own, *came)
    came = [send(part, 1, step) for part, step in zip(away, FAR)]
    near = project(down_weight, came[0], came[1])
    back = [send(part, 1, -step) for part, step in zip(near, FAR[:2])]
    *far, here = project(down_weight, came[2], came[3], here)
    back += [send(part, 1, -step) for part, step in zip(far, FAR[2:])]
    here, *away = add_up(SPANS, here, *back)
    back = [send(part, 0, -step) for part, step in zip(away, FAR)]
    return final_sum(here, *back)


def solution(mesh):
    return jax.shard_map(
        shards,
        mesh=mesh,
        in_specs=(P(("dp", "tensor"), None), P(("dp", "tensor"), None), P("tensor", None)),
        out_specs=P(("dp", "tensor"), None),
        check_vma=False,
    )
```

```python
import jax
import jax.numpy as jnp
import numpy as np
from jax import lax
from jax.experimental import pallas as pl
from jax.experimental.pallas import tpu as pltpu
from jax.sharding import PartitionSpec as P

AXES = ("dp", "tensor")
Z_HI, Y, CORES, Z_LO, X = 4, 8, 2, 4, 4
Z = Z_HI * Z_LO
WIDTH, D, ROWS = 896, 4096, 32
BITS = ((0, 0), (0, 1), (1, 0), (1, 1))
MIB = 1 << 20


def pair_base(value, shift):
    return (value + shift) // 2 * 2 - shift


def squares(outer):
    groups = []
    for zh, y, c, zl, x in np.ndindex(Z_HI, Y, CORES, Z_LO, X):
        z, shift = zh * Z_LO + zl, c ^ outer
        z0, x0 = pair_base(z, shift), pair_base(x, shift)
        if (z0, x0) != (z, x) and (z0 % Z, x0 % X) != (z, x):
            continue
        group = []
        for bz, bx in BITS:
            to_z, to_x = (z0 + bz) % Z, (x0 + bx) % X
            group.append((((to_z // Z_LO * Y + y) * CORES + c) * Z_LO + to_z % Z_LO) * X + to_x)
        groups.append(group)
    return groups


def swap(value, outer):
    return lax.all_to_all(
        value, AXES, split_axis=0, concat_axis=0, axis_index_groups=squares(outer), tiled=True
    )


def vmem(shape):
    return pltpu.VMEM(shape, jnp.bfloat16)


def in_vmem(array):
    return pltpu.with_memory_space_constraint(array, pltpu.VMEM)


def in_hbm(array):
    return pltpu.with_memory_space_constraint(array, pltpu.HBM)


def whole():
    return pl.BlockSpec(memory_space=pltpu.VMEM)


def stays():
    return pl.BlockSpec(memory_space=pltpu.HBM)


def activate_kernel(gate_ref, up_ref, out, gate_buf, up_buf, sems):
    dp, tensor = lax.axis_index("dp"), lax.axis_index("tensor")
    core = lax.rem(dp, CORES)
    zl, x = lax.div(tensor, X), lax.rem(tensor, X)

    def member(value, shift, bit):
        return lax.div(value + shift, 2) * 2 - shift + bit

    copies = []
    for i, (oz, ox) in enumerate(BITS):
        for j, (iz, ix) in enumerate(BITS):
            to_z = member(member(zl + 4, 1 - core, oz), core, iz)
            to_x = member(member(x + 4, 1 - core, ox), core, ix)
            block = lax.rem(to_z, Z_LO) * X + lax.rem(to_x, X)
            columns = pl.ds(pl.multiple_of(block * WIDTH, 128), WIDTH)
            pair = (
                pltpu.make_async_copy(gate_ref.at[:, columns], gate_buf.at[i, j], sems.at[0, i, j]),
                pltpu.make_async_copy(up_ref.at[:, columns], up_buf.at[i, j], sems.at[1, i, j]),
            )
            for copy in pair:
                copy.start()
            copies.append(pair)
    for i in range(4):
        for j in range(4):
            for copy in copies[4 * i + j]:
                copy.wait()
            gate = gate_buf[i, j].astype(jnp.float32)
            out[i, j] = (jax.nn.silu(gate) * up_buf[i, j].astype(jnp.float32)).astype(jnp.bfloat16)


def activate(gate_pre, up_pre):
    shape = (4, 4, ROWS, WIDTH)
    return pl.pallas_call(
        activate_kernel,
        out_shape=vmem(shape),
        in_specs=[stays()] * 2,
        out_specs=whole(),
        scratch_shapes=[
            pltpu.VMEM(shape, jnp.bfloat16),
            pltpu.VMEM(shape, jnp.bfloat16),
            pltpu.SemaphoreType.DMA((2, 4, 4)),
        ],
        compiler_params=pltpu.CompilerParams(vmem_limit_bytes=8 * MIB),
        name="activate",
    )(in_hbm(gate_pre), in_hbm(up_pre))


def regroup_kernel(came, out):
    for i in range(4):
        for j in range(4):
            out[j, ROWS * i : ROWS * (i + 1), :] = came[i, j]


def regroup(came):
    return pl.pallas_call(
        regroup_kernel,
        out_shape=vmem((4, 4 * ROWS, WIDTH)),
        in_specs=[whole()],
        out_specs=whole(),
        compiler_params=pltpu.CompilerParams(vmem_limit_bytes=4 * MIB),
        name="regroup",
    )(in_vmem(came))


TILE = 512
TILES = D // TILE


def project_kernel(hidden, weight, out, held, sems):
    copies = [
        pltpu.make_async_copy(
            weight.at[:, TILE * tile : TILE * (tile + 1)], held.at[tile], sems.at[tile]
        )
        for tile in range(TILES)
    ]
    for copy in copies:
        copy.start()
    rows = hidden[...].reshape(16 * ROWS, WIDTH)
    for tile, copy in enumerate(copies):
        copy.wait()
        terms = jnp.dot(rows, held[tile], preferred_element_type=jnp.float32)
        out[:, :, TILE * tile : TILE * (tile + 1)] = terms.astype(jnp.bfloat16).reshape(4, 4 * ROWS, TILE)


def project(hidden, weight):
    return pl.pallas_call(
        project_kernel,
        out_shape=vmem((4, 4 * ROWS, D)),
        in_specs=[whole(), stays()],
        out_specs=whole(),
        scratch_shapes=[
            pltpu.VMEM((TILES, WIDTH, TILE), jnp.bfloat16),
            pltpu.SemaphoreType.DMA((TILES,)),
        ],
        cost_estimate=pl.CostEstimate(
            flops=2 * 16 * ROWS * WIDTH * D, bytes_accessed=2 * WIDTH * D, transcendentals=0
        ),
        compiler_params=pltpu.CompilerParams(vmem_limit_bytes=16 * MIB),
        name="project",
    )(in_vmem(hidden), in_hbm(weight))


def add_kernel(parts, out):
    @pl.loop(0, TILES)
    def _(tile):
        columns = pl.ds(pl.multiple_of(tile * TILE, TILE), TILE)
        total = parts[0, :, columns].astype(jnp.float32)
        for member in range(1, 4):
            total += parts[member, :, columns].astype(jnp.float32)
        out[:, columns] = total.astype(jnp.bfloat16)


def add_up(parts, out_shape):
    return pl.pallas_call(
        add_kernel,
        out_shape=out_shape,
        in_specs=[whole()],
        out_specs=whole(),
        compiler_params=pltpu.CompilerParams(vmem_limit_bytes=4 * MIB),
        name="add_up",
    )(in_vmem(parts))


def shards(gate_pre, up_pre, down_weight):
    hidden = regroup(swap(activate(gate_pre, up_pre), 1))
    terms = project(swap(hidden, 0), down_weight)
    sums = add_up(swap(terms, 0), vmem((4 * ROWS, D)))
    sums = swap(sums.reshape(4, ROWS, D), 1)
    return add_up(sums, jax.ShapeDtypeStruct((ROWS, D), jnp.bfloat16))


def solution(mesh):
    return jax.shard_map(
        shards,
        mesh=mesh,
        in_specs=(P(("dp", "tensor"), None), P(("dp", "tensor"), None), P("tensor", None)),
        out_specs=P(("dp", "tensor"), None),
        check_vma=False,
    )
```

```python
import functools

import jax
import jax.numpy as jnp
import numpy as np
from jax import lax
from jax.experimental import pallas as pl
from jax.experimental.pallas import tpu as pltpu
from jax.sharding import PartitionSpec as P

AXES = ("dp", "tensor")
Z_HI, Y, CORES, Z_LO, X = 4, 8, 2, 4, 4
Z = Z_HI * Z_LO
WIDTH, D, ROWS = 896, 4096, 32
BITS = ((0, 0), (0, 1), (1, 0), (1, 1))
MIB = 1 << 20


def pair_base(value, shift):
    return (value + shift) // 2 * 2 - shift


def squares(outer):
    groups = []
    for zh, y, c, zl, x in np.ndindex(Z_HI, Y, CORES, Z_LO, X):
        z, shift = zh * Z_LO + zl, c ^ outer
        z0, x0 = pair_base(z, shift), pair_base(x, shift)
        if (z0, x0) != (z, x) and (z0 % Z, x0 % X) != (z, x):
            continue
        group = []
        for bz, bx in BITS:
            to_z, to_x = (z0 + bz) % Z, (x0 + bx) % X
            group.append((((to_z // Z_LO * Y + y) * CORES + c) * Z_LO + to_z % Z_LO) * X + to_x)
        groups.append(group)
    return groups


def swap(value, outer):
    return lax.all_to_all(
        value, AXES, split_axis=0, concat_axis=0, axis_index_groups=squares(outer), tiled=True
    )


def vmem(shape):
    return pltpu.VMEM(shape, jnp.bfloat16)


def in_vmem(array):
    return pltpu.with_memory_space_constraint(array, pltpu.VMEM)


def in_hbm(array):
    return pltpu.with_memory_space_constraint(array, pltpu.HBM)


def whole():
    return pl.BlockSpec(memory_space=pltpu.VMEM)


def stays():
    return pl.BlockSpec(memory_space=pltpu.HBM)


def activate_kernel(gate_ref, up_ref, out, gate_buf, up_buf, sems):
    dp, tensor = lax.axis_index("dp"), lax.axis_index("tensor")
    core = lax.rem(dp, CORES)
    zl, x = lax.div(tensor, X), lax.rem(tensor, X)

    def member(value, shift, bit):
        return lax.div(value + shift, 2) * 2 - shift + bit

    copies = []
    for i, (oz, ox) in enumerate(BITS):
        for j, (iz, ix) in enumerate(BITS):
            to_z = member(member(zl + 4, 1 - core, oz), core, iz)
            to_x = member(member(x + 4, 1 - core, ox), core, ix)
            block = lax.rem(to_z, Z_LO) * X + lax.rem(to_x, X)
            columns = pl.ds(pl.multiple_of(block * WIDTH, 128), WIDTH)
            pair = (
                pltpu.make_async_copy(gate_ref.at[:, columns], gate_buf.at[i, j], sems.at[0, i, j]),
                pltpu.make_async_copy(up_ref.at[:, columns], up_buf.at[i, j], sems.at[1, i, j]),
            )
            for copy in pair:
                copy.start()
            copies.append(pair)
    for i in range(4):
        for j in range(4):
            for copy in copies[4 * i + j]:
                copy.wait()
            gate = gate_buf[i, j].astype(jnp.float32)
            out[i, j] = (jax.nn.silu(gate) * up_buf[i, j].astype(jnp.float32)).astype(jnp.bfloat16)


def activate(gate_pre, up_pre):
    shape = (4, 4, ROWS, WIDTH)
    return pl.pallas_call(
        activate_kernel,
        out_shape=vmem(shape),
        in_specs=[stays()] * 2,
        out_specs=whole(),
        scratch_shapes=[
            pltpu.VMEM(shape, jnp.bfloat16),
            pltpu.VMEM(shape, jnp.bfloat16),
            pltpu.SemaphoreType.DMA((2, 4, 4)),
        ],
        compiler_params=pltpu.CompilerParams(vmem_limit_bytes=8 * MIB),
        name="activate",
    )(in_hbm(gate_pre), in_hbm(up_pre))


def regroup_kernel(came, out):
    for i in range(4):
        for j in range(4):
            out[j, ROWS * i : ROWS * (i + 1), :] = came[i, j]


def regroup(came):
    return pl.pallas_call(
        regroup_kernel,
        out_shape=vmem((4, 4 * ROWS, WIDTH)),
        in_specs=[whole()],
        out_specs=whole(),
        compiler_params=pltpu.CompilerParams(vmem_limit_bytes=4 * MIB),
        name="regroup",
    )(in_vmem(came))


TILE = 512
TILES = D // TILE


def inner_member():
    dp, tensor = lax.axis_index("dp"), lax.axis_index("tensor")
    core = lax.rem(dp, CORES)
    return 2 * lax.rem(lax.div(tensor, X) + core, 2) + lax.rem(lax.rem(tensor, X) + core, 2)


def flip(value, flipped):
    return lax.bitwise_xor(value, jnp.int32(flipped))


def first_terms_kernel(hidden, weight, held, diagonal, sems):
    copies = [
        pltpu.make_async_copy(
            weight.at[:, TILE * tile : TILE * (tile + 1)],
            held.at[:, TILE * tile : TILE * (tile + 1)],
            sems.at[tile],
        )
        for tile in range(TILES)
    ]
    for copy in copies:
        copy.start()
    rows = hidden[flip(inner_member(), 3)]
    for tile, copy in enumerate(copies):
        copy.wait()
        columns = slice(TILE * tile, TILE * (tile + 1))
        diagonal[:, columns] = jnp.dot(
            rows, held[:, columns], preferred_element_type=jnp.float32
        ).astype(jnp.bfloat16)


def first_terms(hidden, weight):
    return pl.pallas_call(
        first_terms_kernel,
        out_shape=[vmem((WIDTH, D)), vmem((4 * ROWS, D))],
        in_specs=[whole(), stays()],
        out_specs=[whole()] * 2,
        scratch_shapes=[pltpu.SemaphoreType.DMA((TILES,))],
        cost_estimate=pl.CostEstimate(flops=1, bytes_accessed=1, transcendentals=0),
        compiler_params=pltpu.CompilerParams(vmem_limit_bytes=4 * MIB),
        name="first_terms",
    )(in_vmem(hidden), in_hbm(weight))


def terms_kernel(flipped, hidden, held, earlier, out):
    del earlier
    rows = hidden[flip(inner_member(), flipped)]
    for tile in range(TILES):
        columns = slice(TILE * tile, TILE * (tile + 1))
        out[:, columns] = jnp.dot(
            rows, held[:, columns], preferred_element_type=jnp.float32
        ).astype(jnp.bfloat16)


def terms_for(hidden, held, flipped, earlier):
    return pl.pallas_call(
        functools.partial(terms_kernel, flipped),
        out_shape=vmem((4 * ROWS, D)),
        in_specs=[whole(), whole(), pl.BlockSpec(memory_space=pl.ANY)],
        out_specs=whole(),
        cost_estimate=pl.CostEstimate(flops=1, bytes_accessed=1, transcendentals=0),
        compiler_params=pltpu.CompilerParams(vmem_limit_bytes=4 * MIB),
        name="terms",
    )(in_vmem(hidden), in_vmem(held), earlier)


def partners(flipped):
    pairs = []
    for group in squares(0):
        pairs += [(group[m], group[m ^ flipped]) for m in range(4)]
    return pairs


def trade(value, flipped):
    return lax.ppermute(value, AXES, partners(flipped))


def add_kernel(*refs):
    *parts, out = refs

    @pl.loop(0, TILES)
    def _(tile):
        columns = pl.ds(pl.multiple_of(tile * TILE, TILE), TILE)
        total = parts[0][:, columns].astype(jnp.float32)
        for part in parts[1:]:
            total += part[:, columns].astype(jnp.float32)
        out[:, columns] = total.astype(out.dtype)


def add(dtype, *parts):
    return pl.pallas_call(
        add_kernel,
        out_shape=pltpu.VMEM((4 * ROWS, D), dtype),
        in_specs=[whole()] * len(parts),
        out_specs=whole(),
        cost_estimate=pl.CostEstimate(flops=1, bytes_accessed=1, transcendentals=0),
        compiler_params=pltpu.CompilerParams(vmem_limit_bytes=4 * MIB),
        name="add",
    )(*(in_vmem(part) for part in parts))


def outer_sum_kernel(parts, out):
    for tile in range(TILES):
        columns = slice(TILE * tile, TILE * (tile + 1))
        total = parts[0, :, columns].astype(jnp.float32)
        for member in range(1, 4):
            total += parts[member, :, columns].astype(jnp.float32)
        out[:, columns] = total.astype(jnp.bfloat16)


def outer_sum(parts):
    return pl.pallas_call(
        outer_sum_kernel,
        out_shape=jax.ShapeDtypeStruct((ROWS, D), jnp.bfloat16),
        in_specs=[whole()],
        out_specs=whole(),
        compiler_params=pltpu.CompilerParams(vmem_limit_bytes=4 * MIB),
        name="outer_sum",
    )(in_vmem(parts))


def shards(gate_pre, up_pre, down_weight):
    hidden = swap(regroup(swap(activate(gate_pre, up_pre), 1)), 0)
    held, diagonal = first_terms(hidden, down_weight)
    beside = terms_for(hidden, held, 1, diagonal)
    below = terms_for(hidden, held, 2, beside)
    own = terms_for(hidden, held, 0, below)
    sums = add(jnp.float32, own, trade(diagonal, 3))
    sums = add(jnp.bfloat16, sums, trade(beside, 1), trade(below, 2))
    return outer_sum(swap(sums.reshape(4, ROWS, D), 1))


def solution(mesh):
    return jax.shard_map(
        shards,
        mesh=mesh,
        in_specs=(P(("dp", "tensor"), None), P(("dp", "tensor"), None), P("tensor", None)),
        out_specs=P(("dp", "tensor"), None),
        check_vma=False,
    )
```

```python
import jax
import jax.numpy as jnp
import numpy as np
from jax import lax
from jax.experimental import pallas as pl
from jax.experimental.pallas import tpu as pltpu
from jax.sharding import PartitionSpec as P

AXES = ("dp", "tensor")
Z_HI, Y, CORES, Z_LO, X = 4, 8, 2, 4, 4
Z = Z_HI * Z_LO
WIDTH, D, ROWS = 896, 4096, 32
BITS = ((0, 0), (0, 1), (1, 0), (1, 1))
MIB = 1 << 20


def pair_base(value, shift):
    return (value + shift) // 2 * 2 - shift


def squares(outer):
    groups = []
    for zh, y, c, zl, x in np.ndindex(Z_HI, Y, CORES, Z_LO, X):
        z, shift = zh * Z_LO + zl, c ^ outer
        z0, x0 = pair_base(z, 1 - shift), pair_base(x, shift)
        if (z0, x0) != (z, x) and (z0 % Z, x0 % X) != (z, x):
            continue
        group = []
        for bz, bx in BITS:
            to_z, to_x = (z0 + bz) % Z, (x0 + bx) % X
            group.append((((to_z // Z_LO * Y + y) * CORES + c) * Z_LO + to_z % Z_LO) * X + to_x)
        groups.append(group)
    return groups


def swap(value, outer):
    return lax.all_to_all(
        value, AXES, split_axis=0, concat_axis=0, axis_index_groups=squares(outer), tiled=True
    )


def vmem(shape):
    return pltpu.VMEM(shape, jnp.bfloat16)


def in_vmem(array):
    return pltpu.with_memory_space_constraint(array, pltpu.VMEM)


def in_hbm(array):
    return pltpu.with_memory_space_constraint(array, pltpu.HBM)


def whole():
    return pl.BlockSpec(memory_space=pltpu.VMEM)


def stays():
    return pl.BlockSpec(memory_space=pltpu.HBM)


def activate_kernel(gate_ref, up_ref, out, gate_buf, up_buf, sems):
    dp, tensor = lax.axis_index("dp"), lax.axis_index("tensor")
    core = lax.rem(dp, CORES)
    zl, x = lax.div(tensor, X), lax.rem(tensor, X)

    def member(value, shift, bit):
        return lax.div(value + shift, 2) * 2 - shift + bit

    copies = []
    for i, (oz, ox) in enumerate(BITS):
        for j, (iz, ix) in enumerate(BITS):
            to_z = member(member(zl + 4, core, oz), 1 - core, iz)
            to_x = member(member(x + 4, 1 - core, ox), core, ix)
            block = lax.rem(to_z, Z_LO) * X + lax.rem(to_x, X)
            columns = pl.ds(pl.multiple_of(block * WIDTH, 128), WIDTH)
            pair = (
                pltpu.make_async_copy(gate_ref.at[:, columns], gate_buf.at[i, j], sems.at[0, i, j]),
                pltpu.make_async_copy(up_ref.at[:, columns], up_buf.at[i, j], sems.at[1, i, j]),
            )
            for copy in pair:
                copy.start()
            copies.append(pair)
    for i in range(4):
        for j in range(4):
            for copy in copies[4 * i + j]:
                copy.wait()
            gate = gate_buf[i, j].astype(jnp.float32)
            out[i, j] = (jax.nn.silu(gate) * up_buf[i, j].astype(jnp.float32)).astype(jnp.bfloat16)


def activate(gate_pre, up_pre):
    shape = (4, 4, ROWS, WIDTH)
    return pl.pallas_call(
        activate_kernel,
        out_shape=vmem(shape),
        in_specs=[stays()] * 2,
        out_specs=whole(),
        scratch_shapes=[
            pltpu.VMEM(shape, jnp.bfloat16),
            pltpu.VMEM(shape, jnp.bfloat16),
            pltpu.SemaphoreType.DMA((2, 4, 4)),
        ],
        compiler_params=pltpu.CompilerParams(vmem_limit_bytes=8 * MIB),
        name="activate",
    )(in_hbm(gate_pre), in_hbm(up_pre))


def inner_member():
    dp, tensor = lax.axis_index("dp"), lax.axis_index("tensor")
    core = lax.rem(dp, CORES)
    return 2 * lax.rem(lax.div(tensor, X) + 1 - core, 2) + lax.rem(lax.rem(tensor, X) + core, 2)


def flip(value, flipped):
    return lax.bitwise_xor(value, jnp.int32(flipped))


def regroup_kernel(came, *outs):
    me = inner_member()
    for flipped, out in enumerate(outs):
        for i in range(4):
            out[ROWS * i : ROWS * (i + 1), :] = came[i, flip(me, flipped)]


def regroup(came):
    return pl.pallas_call(
        regroup_kernel,
        out_shape=[vmem((4 * ROWS, WIDTH))] * 4,
        in_specs=[whole()],
        out_specs=[whole()] * 4,
        compiler_params=pltpu.CompilerParams(vmem_limit_bytes=4 * MIB),
        name="regroup",
    )(in_vmem(came))


TILE = 512
TILES = D // TILE


def first_terms_kernel(rows, weight, held, out, sems):
    copies = [
        pltpu.make_async_copy(
            weight.at[:, TILE * tile : TILE * (tile + 1)],
            held.at[:, TILE * tile : TILE * (tile + 1)],
            sems.at[tile],
        )
        for tile in range(TILES)
    ]
    for copy in copies:
        copy.start()
    for tile, copy in enumerate(copies):
        copy.wait()
        columns = slice(TILE * tile, TILE * (tile + 1))
        out[:, columns] = jnp.dot(
            rows[...], held[:, columns], preferred_element_type=jnp.float32
        ).astype(jnp.bfloat16)


def first_terms(rows, weight):
    return pl.pallas_call(
        first_terms_kernel,
        out_shape=[vmem((WIDTH, D)), vmem((4 * ROWS, D))],
        in_specs=[whole(), stays()],
        out_specs=[whole()] * 2,
        scratch_shapes=[pltpu.SemaphoreType.DMA((TILES,))],
        cost_estimate=pl.CostEstimate(flops=1, bytes_accessed=1, transcendentals=0),
        compiler_params=pltpu.CompilerParams(vmem_limit_bytes=4 * MIB),
        name="first_terms",
    )(in_vmem(rows), in_hbm(weight))


def terms_kernel(rows, held, earlier, out):
    del earlier
    for tile in range(TILES):
        columns = slice(TILE * tile, TILE * (tile + 1))
        out[:, columns] = jnp.dot(
            rows[...], held[:, columns], preferred_element_type=jnp.float32
        ).astype(jnp.bfloat16)


def terms_for(rows, held, earlier):
    return pl.pallas_call(
        terms_kernel,
        out_shape=vmem((4 * ROWS, D)),
        in_specs=[whole(), whole(), pl.BlockSpec(memory_space=pl.ANY)],
        out_specs=whole(),
        cost_estimate=pl.CostEstimate(flops=1, bytes_accessed=1, transcendentals=0),
        compiler_params=pltpu.CompilerParams(vmem_limit_bytes=4 * MIB),
        name="terms",
    )(in_vmem(rows), in_vmem(held), earlier)


def partners(flipped):
    pairs = []
    for group in squares(0):
        pairs += [(group[m], group[m ^ flipped]) for m in range(4)]
    return pairs


def trade(value, flipped):
    return lax.ppermute(value, AXES, partners(flipped))


def add_kernel(*refs):
    *parts, out = refs

    @pl.loop(0, TILES)
    def _(tile):
        columns = pl.ds(pl.multiple_of(tile * TILE, TILE), TILE)
        total = parts[0][:, columns].astype(jnp.float32)
        for part in parts[1:]:
            total += part[:, columns].astype(jnp.float32)
        out[:, columns] = total.astype(out.dtype)


def add(dtype, *parts):
    return pl.pallas_call(
        add_kernel,
        out_shape=pltpu.VMEM((4 * ROWS, D), dtype),
        in_specs=[whole()] * len(parts),
        out_specs=whole(),
        cost_estimate=pl.CostEstimate(flops=1, bytes_accessed=1, transcendentals=0),
        compiler_params=pltpu.CompilerParams(vmem_limit_bytes=4 * MIB),
        name="add",
    )(*(in_vmem(part) for part in parts))


def outer_sum_kernel(parts, out):
    for tile in range(TILES):
        columns = slice(TILE * tile, TILE * (tile + 1))
        total = parts[0, :, columns].astype(jnp.float32)
        for member in range(1, 4):
            total += parts[member, :, columns].astype(jnp.float32)
        out[:, columns] = total.astype(jnp.bfloat16)


def outer_sum(parts):
    return pl.pallas_call(
        outer_sum_kernel,
        out_shape=jax.ShapeDtypeStruct((ROWS, D), jnp.bfloat16),
        in_specs=[whole()],
        out_specs=whole(),
        compiler_params=pltpu.CompilerParams(vmem_limit_bytes=4 * MIB),
        name="outer_sum",
    )(in_vmem(parts))


def shards(gate_pre, up_pre, down_weight):
    own, beside, below, diagonal = regroup(swap(activate(gate_pre, up_pre), 1))
    beside, below, diagonal = trade(beside, 1), trade(below, 2), trade(diagonal, 3)
    held, own = first_terms(own, down_weight)
    diagonal = terms_for(diagonal, held, own)
    beside = terms_for(beside, held, diagonal)
    below = terms_for(below, held, beside)
    sums = add(jnp.float32, own, trade(diagonal, 3))
    sums = add(jnp.bfloat16, sums, trade(beside, 1), trade(below, 2))
    return outer_sum(swap(sums.reshape(4, ROWS, D), 1))


def solution(mesh):
    return jax.shard_map(
        shards,
        mesh=mesh,
        in_specs=(P(("dp", "tensor"), None), P(("dp", "tensor"), None), P("tensor", None)),
        out_specs=P(("dp", "tensor"), None),
        check_vma=False,
    )
```

```python
import jax
import jax.numpy as jnp
import numpy as np
from jax import lax
from jax.experimental import pallas as pl
from jax.experimental.pallas import tpu as pltpu
from jax.sharding import PartitionSpec as P

AXES = ("dp", "tensor")
Z_HI, Y, CORES, Z_LO, X = 4, 8, 2, 4, 4
Z = Z_HI * Z_LO
WIDTH, D, ROWS = 896, 4096, 32
BITS = ((0, 0), (0, 1), (1, 0), (1, 1))
MIB = 1 << 20


def pair_base(value, shift):
    return (value + shift) // 2 * 2 - shift


def squares(outer):
    groups = []
    for zh, y, c, zl, x in np.ndindex(Z_HI, Y, CORES, Z_LO, X):
        z, shift = zh * Z_LO + zl, c ^ outer
        z0, x0 = pair_base(z, 1 - shift), pair_base(x, shift)
        if (z0, x0) != (z, x) and (z0 % Z, x0 % X) != (z, x):
            continue
        group = []
        for bz, bx in BITS:
            to_z, to_x = (z0 + bz) % Z, (x0 + bx) % X
            group.append((((to_z // Z_LO * Y + y) * CORES + c) * Z_LO + to_z % Z_LO) * X + to_x)
        groups.append(group)
    return groups


def swap(value, outer):
    return lax.all_to_all(
        value, AXES, split_axis=0, concat_axis=0, axis_index_groups=squares(outer), tiled=True
    )


def vmem(shape):
    return pltpu.VMEM(shape, jnp.bfloat16)


def in_vmem(array):
    return pltpu.with_memory_space_constraint(array, pltpu.VMEM)


def in_hbm(array):
    return pltpu.with_memory_space_constraint(array, pltpu.HBM)


def whole():
    return pl.BlockSpec(memory_space=pltpu.VMEM)


def stays():
    return pl.BlockSpec(memory_space=pltpu.HBM)


def activate_kernel(gate_ref, up_ref, out, gate_buf, up_buf, sems):
    dp, tensor = lax.axis_index("dp"), lax.axis_index("tensor")
    core = lax.rem(dp, CORES)
    zl, x = lax.div(tensor, X), lax.rem(tensor, X)

    def member(value, shift, bit):
        return lax.div(value + shift, 2) * 2 - shift + bit

    copies = []
    for i, (oz, ox) in enumerate(BITS):
        for j, (iz, ix) in enumerate(BITS):
            to_z = member(member(zl + 4, core, oz), 1 - core, iz)
            to_x = member(member(x + 4, 1 - core, ox), core, ix)
            block = lax.rem(to_z, Z_LO) * X + lax.rem(to_x, X)
            columns = pl.ds(pl.multiple_of(block * WIDTH, 128), WIDTH)
            pair = (
                pltpu.make_async_copy(gate_ref.at[:, columns], gate_buf.at[i, j], sems.at[0, i, j]),
                pltpu.make_async_copy(up_ref.at[:, columns], up_buf.at[i, j], sems.at[1, i, j]),
            )
            for copy in pair:
                copy.start()
            copies.append(pair)
    for i in range(4):
        for j in range(4):
            for copy in copies[4 * i + j]:
                copy.wait()
            gate = gate_buf[i, j].astype(jnp.float32)
            out[i, j] = (jax.nn.silu(gate) * up_buf[i, j].astype(jnp.float32)).astype(jnp.bfloat16)


def activate(gate_pre, up_pre):
    shape = (4, 4, ROWS, WIDTH)
    return pl.pallas_call(
        activate_kernel,
        out_shape=vmem(shape),
        in_specs=[stays()] * 2,
        out_specs=whole(),
        scratch_shapes=[
            pltpu.VMEM(shape, jnp.bfloat16),
            pltpu.VMEM(shape, jnp.bfloat16),
            pltpu.SemaphoreType.DMA((2, 4, 4)),
        ],
        compiler_params=pltpu.CompilerParams(vmem_limit_bytes=8 * MIB),
        name="activate",
    )(in_hbm(gate_pre), in_hbm(up_pre))


def inner_member():
    dp, tensor = lax.axis_index("dp"), lax.axis_index("tensor")
    core = lax.rem(dp, CORES)
    return 2 * lax.rem(lax.div(tensor, X) + 1 - core, 2) + lax.rem(lax.rem(tensor, X) + core, 2)


def flip(value, flipped):
    return lax.bitwise_xor(value, jnp.int32(flipped))


def regroup_kernel(came, *outs):
    me = inner_member()
    for flipped, out in enumerate(outs):
        for i in range(4):
            out[ROWS * i : ROWS * (i + 1), :] = came[i, flip(me, flipped)]


def regroup(came):
    return pl.pallas_call(
        regroup_kernel,
        out_shape=[vmem((4 * ROWS, WIDTH))] * 4,
        in_specs=[whole()],
        out_specs=[whole()] * 4,
        compiler_params=pltpu.CompilerParams(vmem_limit_bytes=4 * MIB),
        name="regroup",
    )(in_vmem(came))


TILE = 512
TILES = D // TILE


def first_terms_kernel(rows, weight, held, out, sems):
    copies = [
        pltpu.make_async_copy(
            weight.at[:, TILE * tile : TILE * (tile + 1)],
            held.at[:, TILE * tile : TILE * (tile + 1)],
            sems.at[tile],
        )
        for tile in range(TILES)
    ]
    for copy in copies:
        copy.start()
    for tile, copy in enumerate(copies):
        copy.wait()
        columns = slice(TILE * tile, TILE * (tile + 1))
        out[:, columns] = jnp.dot(
            rows[...], held[:, columns], preferred_element_type=jnp.float32
        ).astype(jnp.bfloat16)


def first_terms(rows, weight):
    return pl.pallas_call(
        first_terms_kernel,
        out_shape=[vmem((WIDTH, D)), vmem((4 * ROWS, D))],
        in_specs=[whole(), stays()],
        out_specs=[whole()] * 2,
        scratch_shapes=[pltpu.SemaphoreType.DMA((TILES,))],
        cost_estimate=pl.CostEstimate(flops=1, bytes_accessed=1, transcendentals=0),
        compiler_params=pltpu.CompilerParams(vmem_limit_bytes=4 * MIB),
        name="first_terms",
    )(in_vmem(rows), in_hbm(weight))


def terms_kernel(rows, held, earlier, out):
    del earlier
    for tile in range(TILES):
        columns = slice(TILE * tile, TILE * (tile + 1))
        out[:, columns] = jnp.dot(
            rows[...], held[:, columns], preferred_element_type=jnp.float32
        ).astype(jnp.bfloat16)


def terms_for(rows, held, earlier):
    return pl.pallas_call(
        terms_kernel,
        out_shape=vmem((4 * ROWS, D)),
        in_specs=[whole(), whole(), pl.BlockSpec(memory_space=pl.ANY)],
        out_specs=whole(),
        cost_estimate=pl.CostEstimate(flops=1, bytes_accessed=1, transcendentals=0),
        compiler_params=pltpu.CompilerParams(vmem_limit_bytes=4 * MIB),
        name="terms",
    )(in_vmem(rows), in_vmem(held), earlier)


def partners(flipped):
    pairs = []
    for group in squares(0):
        pairs += [(group[m], group[m ^ flipped]) for m in range(4)]
    return pairs


def trade(value, flipped):
    return lax.ppermute(value, AXES, partners(flipped))


def add_kernel(*refs):
    *parts, out = refs

    @pl.loop(0, TILES)
    def _(tile):
        columns = pl.ds(pl.multiple_of(tile * TILE, TILE), TILE)
        total = parts[0][:, columns].astype(jnp.float32)
        for part in parts[1:]:
            total += part[:, columns].astype(jnp.float32)
        out[:, columns] = total.astype(out.dtype)


def add(dtype, *parts):
    return pl.pallas_call(
        add_kernel,
        out_shape=pltpu.VMEM((4 * ROWS, D), dtype),
        in_specs=[whole()] * len(parts),
        out_specs=whole(),
        cost_estimate=pl.CostEstimate(flops=1, bytes_accessed=1, transcendentals=0),
        compiler_params=pltpu.CompilerParams(vmem_limit_bytes=4 * MIB),
        name="add",
    )(*(in_vmem(part) for part in parts))


def outer_sum_kernel(parts, out):
    for tile in range(TILES):
        columns = slice(TILE * tile, TILE * (tile + 1))
        total = parts[0, :, columns].astype(jnp.float32)
        for member in range(1, 4):
            total += parts[member, :, columns].astype(jnp.float32)
        out[:, columns] = total.astype(jnp.bfloat16)


def outer_sum(parts):
    return pl.pallas_call(
        outer_sum_kernel,
        out_shape=jax.ShapeDtypeStruct((ROWS, D), jnp.bfloat16),
        in_specs=[whole()],
        out_specs=whole(),
        compiler_params=pltpu.CompilerParams(vmem_limit_bytes=4 * MIB),
        name="outer_sum",
    )(in_vmem(parts))


def shards(gate_pre, up_pre, down_weight):
    own, beside, below, diagonal = regroup(swap(activate(gate_pre, up_pre), 1))
    diagonal, beside, below = trade(diagonal, 3), trade(beside, 1), trade(below, 2)
    held, diagonal = first_terms(diagonal, down_weight)
    beside = terms_for(beside, held, diagonal)
    below = terms_for(below, held, beside)
    own = terms_for(own, held, below)
    sums = add(jnp.float32, own, trade(diagonal, 3))
    sums = add(jnp.bfloat16, sums, trade(beside, 1), trade(below, 2))
    return outer_sum(swap(sums.reshape(4, ROWS, D), 1))


def solution(mesh):
    return jax.shard_map(
        shards,
        mesh=mesh,
        in_specs=(P(("dp", "tensor"), None), P(("dp", "tensor"), None), P("tensor", None)),
        out_specs=P(("dp", "tensor"), None),
        check_vma=False,
    )
```

```python
import jax
import jax.numpy as jnp
import numpy as np
from jax import lax
from jax.experimental import pallas as pl
from jax.experimental.pallas import tpu as pltpu
from jax.sharding import PartitionSpec as P

AXES = ("dp", "tensor")
Z_HI, Y, CORES, Z_LO, X = 4, 8, 2, 4, 4
Z = Z_HI * Z_LO
WIDTH, D, ROWS = 896, 4096, 32
BITS = ((0, 0), (0, 1), (1, 0), (1, 1))
MIB = 1 << 20


def pair_base(value, shift):
    return (value + shift) // 2 * 2 - shift


def squares(outer):
    groups = []
    for zh, y, c, zl, x in np.ndindex(Z_HI, Y, CORES, Z_LO, X):
        z, shift = zh * Z_LO + zl, c ^ outer
        z0, x0 = pair_base(z, 1 - shift), pair_base(x, shift)
        if (z0, x0) != (z, x) and (z0 % Z, x0 % X) != (z, x):
            continue
        group = []
        for bz, bx in BITS:
            to_z, to_x = (z0 + bz) % Z, (x0 + bx) % X
            group.append((((to_z // Z_LO * Y + y) * CORES + c) * Z_LO + to_z % Z_LO) * X + to_x)
        groups.append(group)
    return groups


def swap(value, outer):
    return lax.all_to_all(
        value, AXES, split_axis=0, concat_axis=0, axis_index_groups=squares(outer), tiled=True
    )


def vmem(shape):
    return pltpu.VMEM(shape, jnp.bfloat16)


def in_vmem(array):
    return pltpu.with_memory_space_constraint(array, pltpu.VMEM)


def in_hbm(array):
    return pltpu.with_memory_space_constraint(array, pltpu.HBM)


def whole():
    return pl.BlockSpec(memory_space=pltpu.VMEM)


def stays():
    return pl.BlockSpec(memory_space=pltpu.HBM)


def activate_kernel(gate_ref, up_ref, out, gate_buf, up_buf, sems):
    dp, tensor = lax.axis_index("dp"), lax.axis_index("tensor")
    core = lax.rem(dp, CORES)
    zl, x = lax.div(tensor, X), lax.rem(tensor, X)

    def member(value, shift, bit):
        return lax.div(value + shift, 2) * 2 - shift + bit

    slabs, copies = [], []
    for oz in range(2):
        for iz in range(2):
            slab = lax.rem(member(member(zl + 4, core, oz), 1 - core, iz), Z_LO)
            columns = pl.ds(pl.multiple_of(slab * X * WIDTH, 128), X * WIDTH)
            place = 2 * oz + iz
            pair = (
                pltpu.make_async_copy(gate_ref.at[:, columns], gate_buf.at[place], sems.at[0, place]),
                pltpu.make_async_copy(up_ref.at[:, columns], up_buf.at[place], sems.at[1, place]),
            )
            for copy in pair:
                copy.start()
            slabs.append((oz, iz))
            copies.append(pair)
    for place, (oz, iz) in enumerate(slabs):
        for copy in copies[place]:
            copy.wait()
        for ox in range(2):
            for ix in range(2):
                block = lax.rem(member(member(x + 4, 1 - core, ox), core, ix), X)
                columns = pl.ds(pl.multiple_of(block * WIDTH, 128), WIDTH)
                gate = gate_buf[place, :, columns].astype(jnp.float32)
                up = up_buf[place, :, columns].astype(jnp.float32)
                out[2 * oz + ox, 2 * iz + ix] = (jax.nn.silu(gate) * up).astype(jnp.bfloat16)


def activate(gate_pre, up_pre):
    shape = (4, 4, ROWS, WIDTH)
    return pl.pallas_call(
        activate_kernel,
        out_shape=vmem(shape),
        in_specs=[stays()] * 2,
        out_specs=whole(),
        scratch_shapes=[
            pltpu.VMEM((4, ROWS, X * WIDTH), jnp.bfloat16),
            pltpu.VMEM((4, ROWS, X * WIDTH), jnp.bfloat16),
            pltpu.SemaphoreType.DMA((2, 4)),
        ],
        compiler_params=pltpu.CompilerParams(vmem_limit_bytes=8 * MIB),
        name="activate",
    )(in_hbm(gate_pre), in_hbm(up_pre))


def inner_member():
    dp, tensor = lax.axis_index("dp"), lax.axis_index("tensor")
    core = lax.rem(dp, CORES)
    return 2 * lax.rem(lax.div(tensor, X) + 1 - core, 2) + lax.rem(lax.rem(tensor, X) + core, 2)


def flip(value, flipped):
    return lax.bitwise_xor(value, jnp.int32(flipped))


def regroup_kernel(came, *outs):
    me = inner_member()
    for flipped, out in enumerate(outs):
        for i in range(4):
            out[ROWS * i : ROWS * (i + 1), :] = came[i, flip(me, flipped)]


def regroup(came):
    return pl.pallas_call(
        regroup_kernel,
        out_shape=[vmem((4 * ROWS, WIDTH))] * 4,
        in_specs=[whole()],
        out_specs=[whole()] * 4,
        compiler_params=pltpu.CompilerParams(vmem_limit_bytes=4 * MIB),
        name="regroup",
    )(in_vmem(came))


TILE = 512
TILES = D // TILE


def first_terms_kernel(rows, weight, held, out, sems):
    copies = [
        pltpu.make_async_copy(
            weight.at[:, TILE * tile : TILE * (tile + 1)],
            held.at[:, TILE * tile : TILE * (tile + 1)],
            sems.at[tile],
        )
        for tile in range(TILES)
    ]
    for copy in copies:
        copy.start()
    for tile, copy in enumerate(copies):
        copy.wait()
        columns = slice(TILE * tile, TILE * (tile + 1))
        out[:, columns] = jnp.dot(
            rows[...], held[:, columns], preferred_element_type=jnp.float32
        ).astype(jnp.bfloat16)


def first_terms(rows, weight):
    return pl.pallas_call(
        first_terms_kernel,
        out_shape=[vmem((WIDTH, D)), vmem((4 * ROWS, D))],
        in_specs=[whole(), stays()],
        out_specs=[whole()] * 2,
        scratch_shapes=[pltpu.SemaphoreType.DMA((TILES,))],
        cost_estimate=pl.CostEstimate(flops=1, bytes_accessed=1, transcendentals=0),
        compiler_params=pltpu.CompilerParams(vmem_limit_bytes=4 * MIB),
        name="first_terms",
    )(in_vmem(rows), in_hbm(weight))


def terms_kernel(rows, held, earlier, out):
    del earlier
    for tile in range(TILES):
        columns = slice(TILE * tile, TILE * (tile + 1))
        out[:, columns] = jnp.dot(
            rows[...], held[:, columns], preferred_element_type=jnp.float32
        ).astype(jnp.bfloat16)


def terms_for(rows, held, earlier):
    return pl.pallas_call(
        terms_kernel,
        out_shape=vmem((4 * ROWS, D)),
        in_specs=[whole(), whole(), pl.BlockSpec(memory_space=pl.ANY)],
        out_specs=whole(),
        cost_estimate=pl.CostEstimate(flops=1, bytes_accessed=1, transcendentals=0),
        compiler_params=pltpu.CompilerParams(vmem_limit_bytes=4 * MIB),
        name="terms",
    )(in_vmem(rows), in_vmem(held), earlier)


def partners(flipped):
    pairs = []
    for group in squares(0):
        pairs += [(group[m], group[m ^ flipped]) for m in range(4)]
    return pairs


def trade(value, flipped):
    return lax.ppermute(value, AXES, partners(flipped))


def add_kernel(*refs):
    *parts, out = refs

    @pl.loop(0, TILES)
    def _(tile):
        columns = pl.ds(pl.multiple_of(tile * TILE, TILE), TILE)
        total = parts[0][:, columns].astype(jnp.float32)
        for part in parts[1:]:
            total += part[:, columns].astype(jnp.float32)
        out[:, columns] = total.astype(out.dtype)


def add(dtype, *parts):
    return pl.pallas_call(
        add_kernel,
        out_shape=pltpu.VMEM((4 * ROWS, D), dtype),
        in_specs=[whole()] * len(parts),
        out_specs=whole(),
        cost_estimate=pl.CostEstimate(flops=1, bytes_accessed=1, transcendentals=0),
        compiler_params=pltpu.CompilerParams(vmem_limit_bytes=4 * MIB),
        name="add",
    )(*(in_vmem(part) for part in parts))


def outer_sum_kernel(parts, out, total, sems):
    half = D // 2
    copies = []
    for side in range(2):
        for tile in range(TILES // 2):
            columns = slice(half * side + TILE * tile, half * side + TILE * (tile + 1))
            terms = parts[0, :, columns].astype(jnp.float32)
            for member in range(1, 4):
                terms += parts[member, :, columns].astype(jnp.float32)
            total[:, columns] = terms.astype(jnp.bfloat16)
        columns = slice(half * side, half * (side + 1))
        copies.append(pltpu.make_async_copy(total.at[:, columns], out.at[:, columns], sems.at[side]))
        copies[-1].start()
    for copy in copies:
        copy.wait()


def outer_sum(parts):
    return pl.pallas_call(
        outer_sum_kernel,
        out_shape=jax.ShapeDtypeStruct((ROWS, D), jnp.bfloat16),
        in_specs=[whole()],
        out_specs=pl.BlockSpec(memory_space=pltpu.HBM),
        scratch_shapes=[pltpu.VMEM((ROWS, D), jnp.bfloat16), pltpu.SemaphoreType.DMA((2,))],
        compiler_params=pltpu.CompilerParams(vmem_limit_bytes=4 * MIB),
        name="outer_sum",
    )(in_vmem(parts))


def shards(gate_pre, up_pre, down_weight):
    own, beside, below, diagonal = regroup(swap(activate(gate_pre, up_pre), 1))
    diagonal, beside, below = trade(diagonal, 3), trade(beside, 1), trade(below, 2)
    held, diagonal = first_terms(diagonal, down_weight)
    beside = terms_for(beside, held, diagonal)
    below = terms_for(below, held, beside)
    own = terms_for(own, held, below)
    sums = add(jnp.float32, own, trade(diagonal, 3))
    sums = add(jnp.bfloat16, sums, trade(beside, 1), trade(below, 2))
    return outer_sum(swap(sums.reshape(4, ROWS, D), 1))


def solution(mesh):
    return jax.shard_map(
        shards,
        mesh=mesh,
        in_specs=(P(("dp", "tensor"), None), P(("dp", "tensor"), None), P("tensor", None)),
        out_specs=P(("dp", "tensor"), None),
        check_vma=False,
    )
```
